32 devices in a mesh: group: 2 (over y), ctx: 4 (over z), head: 2 (over x), req: 2 (over core).
Axes of the slice: x: 2, y: 2, z: 4, core: 2. Of those that a mesh axis runs over, the one named last changes fastest.
Arguments:
- fresh_hidden: bfloat16 [4, 512, 8192], P(('group', 'req'), 'ctx', 'head'), parts along dimension 0, may hold values from -6 to 6
- latent_down: bfloat16 [8192, 512], P('head'), may hold values from -0.0625 to 0.0625
- cache_latents: bfloat16 [4, 1024, 512], P(('group', 'req'), 'ctx', 'head'), parts along dimension 0, may hold values from -6 to 6
- key_up: bfloat16 [2, 256, 128], P('head'), may hold values from -0.375 to 0.375
- value_up: bfloat16 [2, 256, 128], P('head'), may hold values from -0.375 to 0.375
- queries: bfloat16 [4, 512, 2048], P(('group', 'req'), 'ctx', 'head'), parts along dimension 0, may hold values from -160 to 160
- span_start: int32 [4, 4], P(('group', 'req')), parts along dimension 0, may hold values from 0 to 3, as said below
Outputs:
- attention: bfloat16 [4, 512, 2048], P(('group', 'req'), 'ctx', 'head'), parts along dimension 0
The draws below stay inside these ranges and needn't reach their ends.
There are 2 independent parts, one for each index of `group`. The reference program is written for one: setup_inputs(seed, part) draws one part's arguments, and reference() takes and returns one part's arrays. A program takes and returns all parts, laid end to end along the dimension named above; an argument that names none is the same for every part. Nothing has to cross between parts.
Inputs may be any that keep to these rules, and one draw needn't show every extreme that they name: For each request span_start is a permutation of 0 to 4 - 1 over the spans.
All inputs are finite; a program needn't handle non-finite values.
Results may differ from the reference program's by a relative error of at most 0.035.
Values may be sent and summed in bfloat16 or wider, within the bound.
A program may use at most 128 MiB of HBM per device.

```python
import jax
import jax.numpy as jnp
from jax import lax

D = 8192
HD = 128
R = 256
GROUP_Q = 8
FRESH_DEV = 128
CACHE_DEV = 256
KVH = 2
QH = 16
REQS = 2
FRESH = 512
CACHE = 1024
SEQ = 1536
N_CTX = 4


def draw_queries(key, part):
    first_key = jax.random.fold_in(key, 0)
    result = jnp.clip(jax.random.normal(first_key, (REQS, FRESH, QH * HD), jnp.float32), -6.0, 6.0)
    return result.astype(jnp.bfloat16)


def draw_span_start(key, part):
    orders = jnp.stack([jax.random.permutation(jax.random.fold_in(key, 100 + index), N_CTX) for index in range(REQS)])
    return orders.astype(jnp.int32)


def block_scale(rng, shape, cuts, smallest, top_value):
    level, own = 1.0, jax.random.fold_in(rng, 6)
    for position, blocks in cuts:
        heights = jnp.exp(jax.random.uniform(jax.random.fold_in(own, position), (blocks,), jnp.float32, smallest / len(cuts), top_value / len(cuts)))
        level = level * jnp.repeat(heights, shape[position] // blocks).reshape([-1 if axis == position else 1 for axis in range(len(shape))])
    return level


def normal_values(key, dims, scale, bound, cuts=(), held_as=jnp.bfloat16):
    loudness = block_scale(key, dims, cuts, -0.22, 0.18) if cuts else 1.0
    values = jax.random.normal(key, dims, jnp.float32) * scale * loudness
    return jnp.minimum(jnp.maximum(values, -bound), bound).astype(held_as)


def setup_inputs(seed: int = 0, part: int = 0) -> dict:
    seeds = jax.random.split(jax.random.key(seed), 8)
    part_splits = jax.random.split(jax.random.fold_in(seeds[7], part), 8)
    return {
        "fresh_hidden": normal_values(part_splits[0], (REQS, FRESH, D), 1.0, 6.0, ((0, 2), (1, 4), (2, 2))),
        "latent_down": normal_values(seeds[1], (D, 2 * R), D ** -0.5, 0.0625, ((0, 2),)),
        "cache_latents": normal_values(part_splits[2], (REQS, CACHE, 2 * R), 1.0, 6.0, ((0, 2), (1, 4), (2, 2))),
        "key_up": normal_values(seeds[3], (KVH, R, HD), R ** -0.5, 0.375, ((0, 2),)),
        "value_up": normal_values(seeds[4], (KVH, R, HD), R ** -0.5, 0.375, ((0, 2),)),
        "queries": draw_queries(jax.random.fold_in(jax.random.fold_in(seeds[7], part), 71), part),
        "span_start": draw_span_start(jax.random.fold_in(jax.random.fold_in(seeds[7], part), 71), part),
    }


ROPE_BASE = 500000.0
SCORE_FLOOR = -1e30


def rotate(field, positions):
    half_dim = field.shape[-1] // 2
    inv_freq = ROPE_BASE ** (-(jnp.arange(half_dim, dtype=jnp.float32) * 2.0 / field.shape[-1]))
    angles = positions.astype(jnp.float32)[:, None] * inv_freq[None, :]
    cosine = jnp.cos(angles)
    sine_part = jnp.sin(angles)
    first_half = field[..., :half_dim]
    second_half = field[..., half_dim:]
    return jnp.concatenate([first_half * cosine - second_half * sine_part, second_half * cosine + first_half * sine_part], axis=-1)


def reference(fresh_hidden, latent_down, cache_latents, key_up, value_up, queries, span_start):
    score_scale = HD ** -0.5
    results = []
    for request in range(REQS):
        fresh_lat = jnp.dot(fresh_hidden[request], latent_down, preferred_element_type=jnp.float32).astype(jnp.bfloat16)
        latents = jnp.concatenate([cache_latents[request].reshape(N_CTX, CACHE_DEV, 2 * R), fresh_lat.reshape(N_CTX, FRESH_DEV, 2 * R)], axis=1).reshape(SEQ, 2 * R)
        places = span_start[request].astype(jnp.int32)
        cache_pos = places[:, None] * CACHE_DEV + jnp.arange(CACHE_DEV, dtype=jnp.int32)[None, :]
        fresh_pos = CACHE + places[:, None] * FRESH_DEV + jnp.arange(FRESH_DEV, dtype=jnp.int32)[None, :]
        key_pos = jnp.concatenate([cache_pos, fresh_pos], axis=1).reshape(SEQ)
        query_pos = fresh_pos.reshape(FRESH)
        visible = key_pos[None, :] <= query_pos[:, None]
        query_all = queries[request].reshape(FRESH, KVH, GROUP_Q, HD)

        def head_out(kv_index):
            key_rows = rotate(jnp.dot(latents[:, :R], key_up[kv_index], preferred_element_type=jnp.float32), key_pos).astype(jnp.bfloat16)
            value_rows = jnp.dot(latents[:, R:], value_up[kv_index], preferred_element_type=jnp.float32).astype(jnp.bfloat16)

            def one_query_head(member):
                rotated = rotate(query_all[:, kv_index, member, :].astype(jnp.float32), query_pos).astype(jnp.bfloat16)
                scores = jnp.dot(rotated, key_rows.T, preferred_element_type=jnp.float32) * score_scale
                scores = jnp.where(visible, scores, SCORE_FLOOR)
                row_max = jnp.max(scores, axis=1, keepdims=True)
                weights = jnp.where(visible, jnp.exp(scores - row_max), 0.0)
                row_sum = jnp.sum(weights, axis=1)
                mixed_out = jnp.dot(weights.astype(jnp.bfloat16), value_rows, preferred_element_type=jnp.float32) / row_sum[:, None]
                return mixed_out.astype(jnp.bfloat16)

            return lax.map(one_query_head, jnp.arange(GROUP_Q))

        per_head = lax.map(head_out, jnp.arange(KVH))
        results.append(per_head.transpose(2, 0, 1, 3).reshape(FRESH, QH * HD))
    return jnp.stack(results)
```

```python
import functools
import math

import jax
import jax.numpy as jnp
import numpy as np
from jax import lax
from jax.experimental import pallas as pl
from jax.experimental.pallas import tpu as pltpu
from jax.sharding import PartitionSpec as P

ROPE_BASE = 500000.0
SCORE_FLOOR = -1e30
MESH = pl.DeviceIdType.MESH


def rope_tables(span_count, cache_dev, fresh_dev, head_dim):
    half = head_dim // 2
    freq = ROPE_BASE ** (-(np.arange(half, dtype=np.float64) * 2.0 / head_dim))
    freq = np.concatenate([freq, freq])
    sign = np.concatenate([-np.ones(half), np.ones(half)])

    def both(positions):
        angles = positions[:, None].astype(np.float64) * freq[None, :]
        return np.stack([np.cos(angles), np.sin(angles) * sign]).astype(np.float32)

    places = np.arange(span_count)
    near = both(np.arange(max(cache_dev, fresh_dev)))
    far = np.concatenate(
        [both(places * cache_dev), both(span_count * cache_dev + places * fresh_dev)]
    )
    return near, far


def dot(a, b, dims):
    return lax.dot_general(a, b, (dims, ((), ())), preferred_element_type=jnp.float32)


def kernel(
    span_ref, hidden_hbm, down_hbm, cache_ref, kup_ref, vup_ref, q_ref, near_ref, far_ref,
    out_ref,
    hidden, down, crx, part, pout, prx, kvc, kvf, qrot, m_ref, l_ref, acc_ref,
    hsem, dsem, csend, crecv, psend, precv, ssem, rsem,
    *, n, nh, chunks,
):
    c = lax.axis_index("ctx")
    h = lax.axis_index("head")
    fresh_dev = q_ref.shape[1]
    cache_dev, cw = cache_ref.shape[1:]
    rank, hd = kup_ref.shape[1:]
    per_kv = q_ref.shape[2] // hd
    rows = per_kv * fresh_dev
    depth = hidden.shape[1] // chunks
    native = nh == 2 and cw == rank
    loads = []
    for i in range(chunks):
        at = pl.ds(i * depth, depth)
        loads.append((
            pltpu.make_async_copy(hidden_hbm.at[0, :, at], hidden.at[:, at], hsem.at[i]),
            pltpu.make_async_copy(down_hbm.at[at, :], down.at[at, :], dsem.at[i]),
        ))
        for one in loads[-1]:
            one.start()

    barrier = pltpu.get_barrier_semaphore()
    for off in range(1, nh):
        pl.semaphore_signal(
            barrier, inc=1, device_id={"head": lax.rem(h + off, nh)}, device_id_type=MESH
        )

    @pl.when(c > 0)
    def _():
        pl.semaphore_signal(barrier, inc=1, device_id={"ctx": c - 1}, device_id_type=MESH)

    @pl.when(c < n - 1)
    def _():
        pl.semaphore_signal(barrier, inc=1, device_id={"ctx": c + 1}, device_id_type=MESH)

    inner = jnp.where(c > 0, 1, 0) + jnp.where(c < n - 1, 1, 0)
    pl.semaphore_wait(barrier, nh - 1 + inner)

    def to_head(src, dst, send, recv, off):
        return pltpu.make_async_remote_copy(
            src_ref=src, dst_ref=dst.at[h], send_sem=send.at[off], recv_sem=recv.at[h],
            device_id={"head": lax.rem(h + off, nh)}, device_id_type=MESH,
        )

    def from_head(dst, send, recv, off):
        slot = lax.rem(h + nh - off, nh)
        return pltpu.make_async_remote_copy(
            src_ref=dst.at[slot], dst_ref=dst.at[slot], send_sem=send.at[off],
            recv_sem=recv.at[slot], device_id={"head": slot}, device_id_type=MESH,
        )

    for off in range(1, nh):
        to_head(cache_ref.at[0], crx, csend, crecv, off).start()

    def along(piece, span, side):
        ref = kvf.at[span] if piece == 2 else kvc.at[span, piece]
        there = c + 2 * side - 1
        return pltpu.make_async_remote_copy(
            src_ref=ref, dst_ref=ref, send_sem=ssem.at[piece, side, span],
            recv_sem=rsem.at[piece, span], device_id={"ctx": there}, device_id_type=MESH,
        )

    def send_own(piece):
        @pl.when(c > 0)
        def _():
            along(piece, c, 0).start()

        @pl.when(c < n - 1)
        def _():
            along(piece, c, 1).start()

    def turn(table, place):
        row = lax.broadcasted_iota(jnp.int32, (n, hd), 0)
        cos_p = jnp.sum(jnp.where(row == place, far_ref[2 * table], 0.0), axis=0, keepdims=True)
        sin_p = jnp.sum(jnp.where(row == place, far_ref[2 * table + 1], 0.0), axis=0, keepdims=True)
        count = fresh_dev if table else cache_dev
        cos_j = near_ref[0, :count]
        sin_j = near_ref[1, :count]
        return cos_j * cos_p - sin_j * sin_p, sin_j * cos_p + cos_j * sin_p

    def rope(field, cosine, signed_sine):
        return field * cosine + pltpu.roll(field, hd // 2, 1) * signed_sine

    own_place = span_ref[0, c]
    cos_c, sin_c = turn(0, own_place)
    cos_f, sin_f = turn(1, own_place)

    if native:
        @pl.when(h == 0)
        def _():
            raw = dot(cache_ref[0], kup_ref[0], ((1,), (0,)))
            kvc[c, 0] = rope(raw, cos_c, sin_c).astype(jnp.bfloat16)
            send_own(0)

        @pl.when(h == 1)
        def _():
            kvc[c, 1] = dot(cache_ref[0], vup_ref[0], ((1,), (0,))).astype(jnp.bfloat16)
            send_own(1)

    factor = hd ** -0.5 * math.log2(math.e)
    for g in range(per_kv):
        head = q_ref[0, :, g * hd:(g + 1) * hd].astype(jnp.float32)
        qrot[g * fresh_dev:(g + 1) * fresh_dev, :] = (
            rope(head, cos_f, sin_f) * factor
        ).astype(jnp.bfloat16)

    for off in range(1, nh):
        from_head(crx, csend, crecv, off).wait_recv()
    if native:
        @pl.when(h == 1)
        def _():
            raw = dot(crx[0], kup_ref[0], ((1,), (0,)))
            kvc[c, 0] = rope(raw, cos_c, sin_c).astype(jnp.bfloat16)
            send_own(0)

        @pl.when(h == 0)
        def _():
            kvc[c, 1] = dot(crx[1], vup_ref[0], ((1,), (0,))).astype(jnp.bfloat16)
            send_own(1)
    else:
        crx[h] = cache_ref[0]
        raw = jnp.zeros((cache_dev, hd), jnp.float32)
        val = jnp.zeros((cache_dev, hd), jnp.float32)
        for j in range(nh):
            at = j * cw
            if at < rank:
                raw += dot(crx[j], kup_ref[0, at:at + cw], ((1,), (0,)))
            else:
                val += dot(crx[j], vup_ref[0, at - rank:at - rank + cw], ((1,), (0,)))
        kvc[c, 0] = rope(raw, cos_c, sin_c).astype(jnp.bfloat16)
        kvc[c, 1] = val.astype(jnp.bfloat16)
        send_own(0)
        send_own(1)

    for i in range(chunks):
        for one in loads[i]:
            one.wait()
        at = pl.ds(i * depth, depth)
        term = dot(hidden[:, at], down[at, :], ((1,), (0,)))
        if i == 0:
            part[...] = term
        else:
            part[...] += term
    pout[...] = part[...].astype(jnp.bfloat16)
    for off in range(1, nh):
        to_head(pout, prx, psend, precv, off).start()

    def pass_on(piece, step):
        @pl.loop(0, 2)
        def _(side):
            span = c + step - 2 * step * side
            onward = c + 2 * side - 1
            inside = jnp.logical_and(span >= 0, span < n)

            @pl.when(inside)
            def _():
                along(piece, span, side).wait_recv()

                @pl.when(jnp.logical_and(onward >= 0, onward < n))
                def _():
                    along(piece, span, side).start()

    def attend(keys, values, shift):
        val_t = values.T
        width = min(rows, 2 * fresh_dev)
        count = keys.shape[0]

        @pl.loop(0, rows // width)
        def _(i):
            cols = pl.ds(pl.multiple_of(i * width, width), width)
            scores = dot(keys, qrot[cols, :], ((1,), (1,)))
            if shift is not None:
                ik = lax.broadcasted_iota(jnp.int32, (count, width), 0)
                iq = lax.broadcasted_iota(jnp.int32, (count, width), 1)
                iq = jnp.where(iq >= fresh_dev, iq - fresh_dev, iq)
                scores = jnp.where(ik - iq <= shift, scores, SCORE_FLOOR)
            old = m_ref[:, cols]
            new = jnp.maximum(old, jnp.max(scores, axis=0, keepdims=True))
            weights = jnp.exp2(scores - new)
            keep = jnp.exp2(old - new)
            m_ref[:, cols] = new
            l_ref[:, cols] = l_ref[:, cols] * keep + jnp.sum(weights, axis=0, keepdims=True)
            acc_ref[:, cols] = acc_ref[:, cols] * keep + dot(
                val_t, weights.astype(jnp.bfloat16), ((1,), (0,))
            )

    m_ref[...] = jnp.full_like(m_ref, SCORE_FLOOR)
    l_ref[...] = jnp.zeros_like(l_ref)
    acc_ref[...] = jnp.zeros_like(acc_ref)
    pass_on(0, 1)
    pass_on(1, 1)
    attend(kvc[c, 0], kvc[c, 1], None)

    for off in range(1, nh):
        from_head(prx, psend, precv, off).wait_recv()
        slot = lax.rem(h + nh - off, nh)
        part[...] += prx[slot].astype(jnp.float32)
    fresh = part[...].astype(jnp.bfloat16)
    raw = dot(fresh[:, :rank], kup_ref[0], ((1,), (0,)))
    kvf[c, 0] = rope(raw, cos_f, sin_f).astype(jnp.bfloat16)
    kvf[c, 1] = dot(fresh[:, rank:], vup_ref[0], ((1,), (0,))).astype(jnp.bfloat16)
    send_own(2)
    attend(kvf[c, 0], kvf[c, 1], 0)

    @pl.loop(1, n)
    def _(step):
        @pl.when(step > 1)
        def _():
            pass_on(0, step)
            pass_on(1, step)

        @pl.loop(0, 2)
        def _(side):
            span = c + step - 2 * step * side

            @pl.when(jnp.logical_and(span >= 0, span < n))
            def _():
                attend(kvc[span, 0], kvc[span, 1], None)

        pass_on(2, step)

        @pl.loop(0, 2)
        def _(side):
            span = c + step - 2 * step * side

            @pl.when(jnp.logical_and(span >= 0, span < n))
            def _():
                attend(kvf[span, 0], kvf[span, 1], (own_place - span_ref[0, span]) * fresh_dev)

    for g in range(per_kv):
        cols = slice(g * fresh_dev, (g + 1) * fresh_dev)
        mixed = acc_ref[:, cols] / l_ref[:, cols]
        out_ref[0, :, g * hd:(g + 1) * hd] = mixed.T.astype(out_ref.dtype)

    for off in range(1, nh):
        to_head(cache_ref.at[0], crx, csend, crecv, off).wait_send()
        to_head(pout, prx, psend, precv, off).wait_send()

    @pl.loop(0, n)
    def _(span):
        for piece in range(3):
            @pl.when(jnp.logical_and(span >= c, c > 0))
            def _():
                along(piece, span, 0).wait_send()

            @pl.when(jnp.logical_and(span <= c, c < n - 1))
            def _():
                along(piece, span, 1).wait_send()


def per_device(n, nh, fresh_hidden, latent_down, cache_latents, key_up, value_up, queries, span_start):
    fresh_dev, depth = fresh_hidden.shape[1:]
    cache_dev, cw = cache_latents.shape[1:]
    lat = latent_down.shape[1]
    hd = key_up.shape[2]
    rows = fresh_dev * (queries.shape[2] // hd)
    near, far = rope_tables(n, cache_dev, fresh_dev, hd)
    chunks = 4
    vmem = pl.BlockSpec(memory_space=pltpu.VMEM)
    hbm = pl.BlockSpec(memory_space=pl.ANY)
    dma = pltpu.SemaphoreType.DMA
    bf = jnp.bfloat16
    return pl.pallas_call(
        functools.partial(kernel, n=n, nh=nh, chunks=chunks),
        out_shape=jax.ShapeDtypeStruct(queries.shape, queries.dtype),
        in_specs=[pl.BlockSpec(memory_space=pltpu.SMEM), hbm, hbm] + [vmem] * 6,
        out_specs=vmem,
        scratch_shapes=[
            pltpu.VMEM((fresh_dev, depth), bf),
            pltpu.VMEM((depth, lat), bf),
            pltpu.VMEM((nh, cache_dev, cw), bf),
            pltpu.VMEM((fresh_dev, lat), jnp.float32),
            pltpu.VMEM((fresh_dev, lat), bf),
            pltpu.VMEM((nh, fresh_dev, lat), bf),
            pltpu.VMEM((n, 2, cache_dev, hd), bf),
            pltpu.VMEM((n, 2, fresh_dev, hd), bf),
            pltpu.VMEM((rows, hd), bf),
            pltpu.VMEM((1, rows), jnp.float32),
            pltpu.VMEM((1, rows), jnp.float32),
            pltpu.VMEM((hd, rows), jnp.float32),
            dma((chunks,)), dma((chunks,)),
            dma((nh,)), dma((nh,)), dma((nh,)), dma((nh,)),
            dma((3, 2, n)), dma((3, n)),
        ],
        compiler_params=pltpu.CompilerParams(
            collective_id=0, has_side_effects=True, vmem_limit_bytes=40 * 2 ** 20
        ),
    )(span_start, fresh_hidden, latent_down, cache_latents, key_up, value_up, queries,
      jnp.asarray(near), jnp.asarray(far))


def solution(mesh):
    return jax.shard_map(
        functools.partial(per_device, mesh.shape["ctx"], mesh.shape["head"]),
        mesh=mesh,
        in_specs=(
            P(("group", "req"), "ctx", "head"),
            P("head", None),
            P(("group", "req"), "ctx", "head"),
            P("head", None, None),
            P("head", None, None),
            P(("group", "req"), "ctx", "head"),
            P(("group", "req"), None),
        ),
        out_specs=P(("group", "req"), "ctx", "head"),
        check_vma=False,
    )
```

```python
import functools
import math

import jax
import jax.numpy as jnp
import numpy as np
from jax import lax
from jax.experimental import pallas as pl
from jax.experimental.pallas import tpu as pltpu
from jax.sharding import PartitionSpec as P

ROPE_BASE = 500000.0
SCORE_FLOOR = -1e30
MESH = pl.DeviceIdType.MESH


def rope_tables(span_count, cache_dev, fresh_dev, head_dim):
    half = head_dim // 2
    freq = ROPE_BASE ** (-(np.arange(half, dtype=np.float64) * 2.0 / head_dim))
    freq = np.concatenate([freq, freq])
    sign = np.concatenate([-np.ones(half), np.ones(half)])

    def both(positions):
        angles = positions[:, None].astype(np.float64) * freq[None, :]
        return np.stack([np.cos(angles), np.sin(angles) * sign]).astype(np.float32)

    places = np.arange(span_count)
    near = both(np.arange(max(cache_dev, fresh_dev)))
    far = np.concatenate(
        [both(places * cache_dev), both(span_count * cache_dev + places * fresh_dev)]
    )
    return near, far


def dot(a, b, dims):
    return lax.dot_general(a, b, (dims, ((), ())), preferred_element_type=jnp.float32)


def kernel(
    span_ref, hidden_hbm, down_hbm, cache_hbm, kup_hbm, vup_hbm, q_hbm, near_hbm, far_hbm,
    out_ref,
    cache_ref, kup_ref, vup_ref, q_ref, near_ref, far_ref, isem, hidden, down, crx, part, pout, prx, kvc, kvf, qrot, m_ref, l_ref, acc_ref,
    hsem, dsem, csend, crecv, psend, precv, ssem, rsem,
    *, n, nh, chunks,
):
    c = lax.axis_index("ctx")
    h = lax.axis_index("head")
    fresh_dev = q_ref.shape[1]
    cache_dev, cw = cache_ref.shape[1:]
    rank, hd = kup_ref.shape[1:]
    per_kv = q_ref.shape[2] // hd
    rows = per_kv * fresh_dev
    depth = hidden.shape[1] // chunks
    native = nh == 2 and cw == rank
    small = [
        pltpu.make_async_copy(src, dst, isem.at[i])
        for i, (src, dst) in enumerate((
            (cache_hbm, cache_ref), (kup_hbm, kup_ref), (vup_hbm, vup_ref),
            (near_hbm, near_ref), (far_hbm, far_ref), (q_hbm, q_ref),
        ))
    ]
    for one in small:
        one.start()
    loads = []
    for i in range(chunks):
        at = pl.ds(i * depth, depth)
        loads.append((
            pltpu.make_async_copy(hidden_hbm.at[0, :, at], hidden.at[:, at], hsem.at[i]),
            pltpu.make_async_copy(down_hbm.at[at, :], down.at[at, :], dsem.at[i]),
        ))
        for one in loads[-1]:
            one.start()

    barrier = pltpu.get_barrier_semaphore()
    for off in range(1, nh):
        pl.semaphore_signal(
            barrier, inc=1, device_id={"head": lax.rem(h + off, nh)}, device_id_type=MESH
        )

    @pl.when(c > 0)
    def _():
        pl.semaphore_signal(barrier, inc=1, device_id={"ctx": c - 1}, device_id_type=MESH)

    @pl.when(c < n - 1)
    def _():
        pl.semaphore_signal(barrier, inc=1, device_id={"ctx": c + 1}, device_id_type=MESH)

    inner = jnp.where(c > 0, 1, 0) + jnp.where(c < n - 1, 1, 0)
    pl.semaphore_wait(barrier, nh - 1 + inner)

    def to_head(src, dst, send, recv, off):
        return pltpu.make_async_remote_copy(
            src_ref=src, dst_ref=dst.at[h], send_sem=send.at[off], recv_sem=recv.at[h],
            device_id={"head": lax.rem(h + off, nh)}, device_id_type=MESH,
        )

    def from_head(dst, send, recv, off):
        slot = lax.rem(h + nh - off, nh)
        return pltpu.make_async_remote_copy(
            src_ref=dst.at[slot], dst_ref=dst.at[slot], send_sem=send.at[off],
            recv_sem=recv.at[slot], device_id={"head": slot}, device_id_type=MESH,
        )

    small[0].wait()
    for off in range(1, nh):
        to_head(cache_ref.at[0], crx, csend, crecv, off).start()

    def along(piece, span, side):
        ref = kvf.at[span] if piece == 2 else kvc.at[span, piece]
        there = c + 2 * side - 1
        return pltpu.make_async_remote_copy(
            src_ref=ref, dst_ref=ref, send_sem=ssem.at[piece, side, span],
            recv_sem=rsem.at[piece, span], device_id={"ctx": there}, device_id_type=MESH,
        )

    def send_own(piece):
        @pl.when(c > 0)
        def _():
            along(piece, c, 0).start()

        @pl.when(c < n - 1)
        def _():
            along(piece, c, 1).start()

    def turn(table, place):
        row = lax.broadcasted_iota(jnp.int32, (n, hd), 0)
        cos_p = jnp.sum(jnp.where(row == place, far_ref[2 * table], 0.0), axis=0, keepdims=True)
        sin_p = jnp.sum(jnp.where(row == place, far_ref[2 * table + 1], 0.0), axis=0, keepdims=True)
        count = fresh_dev if table else cache_dev
        cos_j = near_ref[0, :count]
        sin_j = near_ref[1, :count]
        return cos_j * cos_p - sin_j * sin_p, sin_j * cos_p + cos_j * sin_p

    def rope(field, cosine, signed_sine):
        return field * cosine + pltpu.roll(field, hd // 2, 1) * signed_sine

    for one in small[1:5]:
        one.wait()
    own_place = span_ref[0, c]
    cos_c, sin_c = turn(0, own_place)
    cos_f, sin_f = turn(1, own_place)

    if native:
        @pl.when(h == 0)
        def _():
            raw = dot(cache_ref[0], kup_ref[0], ((1,), (0,)))
            kvc[c, 0] = rope(raw, cos_c, sin_c).astype(jnp.bfloat16)
            send_own(0)

        @pl.when(h == 1)
        def _():
            kvc[c, 1] = dot(cache_ref[0], vup_ref[0], ((1,), (0,))).astype(jnp.bfloat16)
            send_own(1)

    small[5].wait()
    factor = hd ** -0.5 * math.log2(math.e)
    for g in range(per_kv):
        head = q_ref[0, :, g * hd:(g + 1) * hd].astype(jnp.float32)
        qrot[g * fresh_dev:(g + 1) * fresh_dev, :] = (
            rope(head, cos_f, sin_f) * factor
        ).astype(jnp.bfloat16)

    for off in range(1, nh):
        from_head(crx, csend, crecv, off).wait_recv()
    if native:
        @pl.when(h == 1)
        def _():
            raw = dot(crx[0], kup_ref[0], ((1,), (0,)))
            kvc[c, 0] = rope(raw, cos_c, sin_c).astype(jnp.bfloat16)
            send_own(0)

        @pl.when(h == 0)
        def _():
            kvc[c, 1] = dot(crx[1], vup_ref[0], ((1,), (0,))).astype(jnp.bfloat16)
            send_own(1)
    else:
        crx[h] = cache_ref[0]
        raw = jnp.zeros((cache_dev, hd), jnp.float32)
        val = jnp.zeros((cache_dev, hd), jnp.float32)
        for j in range(nh):
            at = j * cw
            if at < rank:
                raw += dot(crx[j], kup_ref[0, at:at + cw], ((1,), (0,)))
            else:
                val += dot(crx[j], vup_ref[0, at - rank:at - rank + cw], ((1,), (0,)))
        kvc[c, 0] = rope(raw, cos_c, sin_c).astype(jnp.bfloat16)
        kvc[c, 1] = val.astype(jnp.bfloat16)
        send_own(0)
        send_own(1)

    for i in range(chunks):
        for one in loads[i]:
            one.wait()
        at = pl.ds(i * depth, depth)
        term = dot(hidden[:, at], down[at, :], ((1,), (0,)))
        if i == 0:
            part[...] = term
        else:
            part[...] += term
    pout[...] = part[...].astype(jnp.bfloat16)
    for off in range(1, nh):
        to_head(pout, prx, psend, precv, off).start()

    def pass_on(piece, step):
        @pl.loop(0, 2)
        def _(side):
            span = c + step - 2 * step * side
            onward = c + 2 * side - 1
            inside = jnp.logical_and(span >= 0, span < n)

            @pl.when(inside)
            def _():
                along(piece, span, side).wait_recv()

                @pl.when(jnp.logical_and(onward >= 0, onward < n))
                def _():
                    along(piece, span, side).start()

    def attend(keys, values, shift):
        val_t = values.T
        width = min(rows, 2 * fresh_dev)
        count = keys.shape[0]

        @pl.loop(0, rows // width)
        def _(i):
            cols = pl.ds(pl.multiple_of(i * width, width), width)
            scores = dot(keys, qrot[cols, :], ((1,), (1,)))
            if shift is not None:
                ik = lax.broadcasted_iota(jnp.int32, (count, width), 0)
                iq = lax.broadcasted_iota(jnp.int32, (count, width), 1)
                iq = jnp.where(iq >= fresh_dev, iq - fresh_dev, iq)
                scores = jnp.where(ik - iq <= shift, scores, SCORE_FLOOR)
            old = m_ref[:, cols]
            new = jnp.maximum(old, jnp.max(scores, axis=0, keepdims=True))
            weights = jnp.exp2(scores - new)
            keep = jnp.exp2(old - new)
            m_ref[:, cols] = new
            l_ref[:, cols] = l_ref[:, cols] * keep + jnp.sum(weights, axis=0, keepdims=True)
            acc_ref[:, cols] = acc_ref[:, cols] * keep + dot(
                val_t, weights.astype(jnp.bfloat16), ((1,), (0,))
            )

    m_ref[...] = jnp.full_like(m_ref, SCORE_FLOOR)
    l_ref[...] = jnp.zeros_like(l_ref)
    acc_ref[...] = jnp.zeros_like(acc_ref)
    pass_on(0, 1)
    pass_on(1, 1)
    attend(kvc[c, 0], kvc[c, 1], None)

    for off in range(1, nh):
        from_head(prx, psend, precv, off).wait_recv()
        slot = lax.rem(h + nh - off, nh)
        part[...] += prx[slot].astype(jnp.float32)
    fresh = part[...].astype(jnp.bfloat16)
    raw = dot(fresh[:, :rank], kup_ref[0], ((1,), (0,)))
    kvf[c, 0] = rope(raw, cos_f, sin_f).astype(jnp.bfloat16)
    kvf[c, 1] = dot(fresh[:, rank:], vup_ref[0], ((1,), (0,))).astype(jnp.bfloat16)
    send_own(2)
    attend(kvf[c, 0], kvf[c, 1], 0)

    @pl.loop(1, n)
    def _(step):
        @pl.when(step > 1)
        def _():
            pass_on(0, step)
            pass_on(1, step)

        @pl.loop(0, 2)
        def _(side):
            span = c + step - 2 * step * side

            @pl.when(jnp.logical_and(span >= 0, span < n))
            def _():
                attend(kvc[span, 0], kvc[span, 1], None)

        pass_on(2, step)

        @pl.loop(0, 2)
        def _(side):
            span = c + step - 2 * step * side

            @pl.when(jnp.logical_and(span >= 0, span < n))
            def _():
                attend(kvf[span, 0], kvf[span, 1], (own_place - span_ref[0, span]) * fresh_dev)

    for g in range(per_kv):
        cols = slice(g * fresh_dev, (g + 1) * fresh_dev)
        mixed = acc_ref[:, cols] / l_ref[:, cols]
        out_ref[0, :, g * hd:(g + 1) * hd] = mixed.T.astype(out_ref.dtype)

    for off in range(1, nh):
        to_head(cache_ref.at[0], crx, csend, crecv, off).wait_send()
        to_head(pout, prx, psend, precv, off).wait_send()

    @pl.loop(0, n)
    def _(span):
        for piece in range(3):
            @pl.when(jnp.logical_and(span >= c, c > 0))
            def _():
                along(piece, span, 0).wait_send()

            @pl.when(jnp.logical_and(span <= c, c < n - 1))
            def _():
                along(piece, span, 1).wait_send()


def per_device(n, nh, fresh_hidden, latent_down, cache_latents, key_up, value_up, queries, span_start):
    fresh_dev, depth = fresh_hidden.shape[1:]
    cache_dev, cw = cache_latents.shape[1:]
    lat = latent_down.shape[1]
    hd = key_up.shape[2]
    rows = fresh_dev * (queries.shape[2] // hd)
    near, far = rope_tables(n, cache_dev, fresh_dev, hd)
    near, far = jnp.asarray(near), jnp.asarray(far)
    small = (cache_latents, key_up, value_up, queries, near, far)
    chunks = 4
    vmem = pl.BlockSpec(memory_space=pltpu.VMEM)
    hbm = pl.BlockSpec(memory_space=pltpu.HBM)
    dma = pltpu.SemaphoreType.DMA
    bf = jnp.bfloat16
    return pl.pallas_call(
        functools.partial(kernel, n=n, nh=nh, chunks=chunks),
        out_shape=jax.ShapeDtypeStruct(queries.shape, queries.dtype),
        in_specs=[pl.BlockSpec(memory_space=pltpu.SMEM)] + [hbm] * 8,
        out_specs=vmem,
        scratch_shapes=[
            *(pltpu.VMEM(x.shape, x.dtype) for x in small),
            dma((len(small),)),
            pltpu.VMEM((fresh_dev, depth), bf),
            pltpu.VMEM((depth, lat), bf),
            pltpu.VMEM((nh, cache_dev, cw), bf),
            pltpu.VMEM((fresh_dev, lat), jnp.float32),
            pltpu.VMEM((fresh_dev, lat), bf),
            pltpu.VMEM((nh, fresh_dev, lat), bf),
            pltpu.VMEM((n, 2, cache_dev, hd), bf),
            pltpu.VMEM((n, 2, fresh_dev, hd), bf),
            pltpu.VMEM((rows, hd), bf),
            pltpu.VMEM((1, rows), jnp.float32),
            pltpu.VMEM((1, rows), jnp.float32),
            pltpu.VMEM((hd, rows), jnp.float32),
            dma((chunks,)), dma((chunks,)),
            dma((nh,)), dma((nh,)), dma((nh,)), dma((nh,)),
            dma((3, 2, n)), dma((3, n)),
        ],
        compiler_params=pltpu.CompilerParams(
            collective_id=0, has_side_effects=True, vmem_limit_bytes=62 * 2 ** 20
        ),
    )(span_start, fresh_hidden, latent_down, cache_latents, key_up, value_up, queries,
      near, far)


def solution(mesh):
    return jax.shard_map(
        functools.partial(per_device, mesh.shape["ctx"], mesh.shape["head"]),
        mesh=mesh,
        in_specs=(
            P(("group", "req"), "ctx", "head"),
            P("head", None),
            P(("group", "req"), "ctx", "head"),
            P("head", None, None),
            P("head", None, None),
            P(("group", "req"), "ctx", "head"),
            P(("group", "req"), None),
        ),
        out_specs=P(("group", "req"), "ctx", "head"),
        check_vma=False,
    )
```

```python
import functools
import math

import jax
import jax.numpy as jnp
import numpy as np
from jax import lax
from jax.experimental import pallas as pl
from jax.experimental.pallas import tpu as pltpu
from jax.sharding import PartitionSpec as P

ROPE_BASE = 500000.0
SCORE_FLOOR = -1e30
MESH = pl.DeviceIdType.MESH


def rope_tables(span_count, cache_dev, fresh_dev, head_dim):
    half = head_dim // 2
    freq = ROPE_BASE ** (-(np.arange(half, dtype=np.float64) * 2.0 / head_dim))
    freq = np.concatenate([freq, freq])
    sign = np.concatenate([-np.ones(half), np.ones(half)])

    def both(positions):
        angles = positions[:, None].astype(np.float64) * freq[None, :]
        return np.stack([np.cos(angles), np.sin(angles) * sign]).astype(np.float32)

    places = np.arange(span_count)
    near = both(np.arange(max(cache_dev, fresh_dev)))
    far = np.concatenate(
        [both(places * cache_dev), both(span_count * cache_dev + places * fresh_dev)]
    )
    return near, far


def dot(a, b, dims):
    return lax.dot_general(a, b, (dims, ((), ())), preferred_element_type=jnp.float32)


def kernel(
    span_ref, hidden_hbm, down_hbm, cache_hbm, kup_hbm, vup_hbm, q_hbm, near_hbm, far_hbm,
    out_ref,
    cache_ref, kup_ref, vup_ref, q_ref, near_ref, far_ref, isem, hidden, down, crx, part, pout, prx, kvc, kvf, qrot, m_ref, l_ref, acc_ref,
    hsem, dsem, csend, crecv, psend, precv, ssem, rsem,
    *, n, nh, chunks,
):
    c = lax.axis_index("ctx")
    h = lax.axis_index("head")
    fresh_dev = q_ref.shape[1]
    cache_dev, cw = cache_ref.shape[1:]
    rank, hd = kup_ref.shape[1:]
    per_kv = q_ref.shape[2] // hd
    rows = per_kv * fresh_dev
    depth = hidden.shape[1] // chunks
    native = nh == 2 and cw == rank
    small = [
        pltpu.make_async_copy(src, dst, isem.at[i])
        for i, (src, dst) in enumerate((
            (cache_hbm, cache_ref), (kup_hbm, kup_ref), (vup_hbm, vup_ref),
            (near_hbm, near_ref), (far_hbm, far_ref), (q_hbm, q_ref),
        ))
    ]
    for one in small:
        one.start()
    loads = []
    for i in range(chunks):
        at = pl.ds(i * depth, depth)
        loads.append((
            pltpu.make_async_copy(hidden_hbm.at[0, :, at], hidden.at[:, at], hsem.at[i]),
            pltpu.make_async_copy(down_hbm.at[at, :], down.at[at, :], dsem.at[i]),
        ))
        for one in loads[-1]:
            one.start()

    barrier = pltpu.get_barrier_semaphore()
    for off in range(1, nh):
        pl.semaphore_signal(
            barrier, inc=1, device_id={"head": lax.rem(h + off, nh)}, device_id_type=MESH
        )

    @pl.when(c > 0)
    def _():
        pl.semaphore_signal(barrier, inc=1, device_id={"ctx": c - 1}, device_id_type=MESH)

    @pl.when(c < n - 1)
    def _():
        pl.semaphore_signal(barrier, inc=1, device_id={"ctx": c + 1}, device_id_type=MESH)

    inner = jnp.where(c > 0, 1, 0) + jnp.where(c < n - 1, 1, 0)
    pl.semaphore_wait(barrier, nh - 1 + inner)

    def to_head(src, dst, send, recv, off):
        return pltpu.make_async_remote_copy(
            src_ref=src, dst_ref=dst.at[h], send_sem=send.at[off], recv_sem=recv.at[h],
            device_id={"head": lax.rem(h + off, nh)}, device_id_type=MESH,
        )

    def from_head(dst, send, recv, off):
        slot = lax.rem(h + nh - off, nh)
        return pltpu.make_async_remote_copy(
            src_ref=dst.at[slot], dst_ref=dst.at[slot], send_sem=send.at[off],
            recv_sem=recv.at[slot], device_id={"head": slot}, device_id_type=MESH,
        )

    small[0].wait()
    for off in range(1, nh):
        to_head(cache_ref.at[0], crx, csend, crecv, off).start()

    def along(piece, span, side):
        ref = kvf.at[span] if isinstance(piece, int) and piece == 2 else kvc.at[span, piece]
        there = c + 2 * side - 1
        return pltpu.make_async_remote_copy(
            src_ref=ref, dst_ref=ref, send_sem=ssem.at[piece, side, span],
            recv_sem=rsem.at[piece, span], device_id={"ctx": there}, device_id_type=MESH,
        )

    def send_own(piece):
        @pl.when(c > 0)
        def _():
            along(piece, c, 0).start()

        @pl.when(c < n - 1)
        def _():
            along(piece, c, 1).start()

    def turn(table, place):
        row = lax.broadcasted_iota(jnp.int32, (n, hd), 0)
        cos_p = jnp.sum(jnp.where(row == place, far_ref[2 * table], 0.0), axis=0, keepdims=True)
        sin_p = jnp.sum(jnp.where(row == place, far_ref[2 * table + 1], 0.0), axis=0, keepdims=True)
        count = fresh_dev if table else cache_dev
        cos_j = near_ref[0, :count]
        sin_j = near_ref[1, :count]
        return cos_j * cos_p - sin_j * sin_p, sin_j * cos_p + cos_j * sin_p

    def rope(field, cosine, signed_sine):
        return field * cosine + pltpu.roll(field, hd // 2, 1) * signed_sine

    for one in small[1:5]:
        one.wait()
    own_place = span_ref[0, c]
    cos_c, sin_c = turn(0, own_place)
    cos_f, sin_f = turn(1, own_place)

    if native:
        @pl.when(h == 0)
        def _():
            raw = dot(cache_ref[0], kup_ref[0], ((1,), (0,)))
            kvc[c, 0] = rope(raw, cos_c, sin_c).astype(jnp.bfloat16)
            send_own(0)

        @pl.when(h == 1)
        def _():
            kvc[c, 1] = dot(cache_ref[0], vup_ref[0], ((1,), (0,))).astype(jnp.bfloat16)
            send_own(1)

    for i in range(chunks):
        for one in loads[i]:
            one.wait()
        at = pl.ds(i * depth, depth)
        term = dot(hidden[:, at], down[at, :], ((1,), (0,)))
        if i == 0:
            part[...] = term
        else:
            part[...] += term
    pout[...] = part[...].astype(jnp.bfloat16)
    for off in range(1, nh):
        to_head(pout, prx, psend, precv, off).start()

    for off in range(1, nh):
        from_head(crx, csend, crecv, off).wait_recv()
    if native:
        @pl.when(h == 1)
        def _():
            raw = dot(crx[0], kup_ref[0], ((1,), (0,)))
            kvc[c, 0] = rope(raw, cos_c, sin_c).astype(jnp.bfloat16)
            send_own(0)

        @pl.when(h == 0)
        def _():
            kvc[c, 1] = dot(crx[1], vup_ref[0], ((1,), (0,))).astype(jnp.bfloat16)
            send_own(1)
    else:
        crx[h] = cache_ref[0]
        raw = jnp.zeros((cache_dev, hd), jnp.float32)
        val = jnp.zeros((cache_dev, hd), jnp.float32)
        for j in range(nh):
            at = j * cw
            if at < rank:
                raw += dot(crx[j], kup_ref[0, at:at + cw], ((1,), (0,)))
            else:
                val += dot(crx[j], vup_ref[0, at - rank:at - rank + cw], ((1,), (0,)))
        kvc[c, 0] = rope(raw, cos_c, sin_c).astype(jnp.bfloat16)
        kvc[c, 1] = val.astype(jnp.bfloat16)
        send_own(0)
        send_own(1)

    small[5].wait()
    factor = hd ** -0.5 * math.log2(math.e)
    for g in range(per_kv):
        head = q_ref[0, :, g * hd:(g + 1) * hd].astype(jnp.float32)
        qrot[g * fresh_dev:(g + 1) * fresh_dev, :] = (
            rope(head, cos_f, sin_f) * factor
        ).astype(jnp.bfloat16)

    def pass_on(piece, step):
        @pl.loop(0, 2)
        def _(side):
            span = c + step - 2 * step * side
            onward = c + 2 * side - 1
            inside = jnp.logical_and(span >= 0, span < n)

            @pl.when(inside)
            def _():
                along(piece, span, side).wait_recv()

                @pl.when(jnp.logical_and(onward >= 0, onward < n))
                def _():
                    along(piece, span, side).start()

    def attend(keys, values, shift):
        val_t = values.T
        width = min(rows, 2 * fresh_dev)
        count = keys.shape[0]

        @pl.loop(0, rows // width, unroll=True)
        def _(i):
            cols = pl.ds(pl.multiple_of(i * width, width), width)
            scores = dot(keys, qrot[cols, :], ((1,), (1,)))
            if shift is not None:
                ik = lax.broadcasted_iota(jnp.int32, (count, width), 0)
                iq = lax.broadcasted_iota(jnp.int32, (count, width), 1)
                iq = jnp.where(iq >= fresh_dev, iq - fresh_dev, iq)
                scores = jnp.where(ik - iq <= shift, scores, SCORE_FLOOR)
            old = m_ref[:, cols]
            new = jnp.maximum(old, jnp.max(scores, axis=0, keepdims=True))
            weights = jnp.exp2(scores - new)
            keep = jnp.exp2(old - new)
            m_ref[:, cols] = new
            l_ref[:, cols] = l_ref[:, cols] * keep + jnp.sum(weights, axis=0, keepdims=True)
            acc_ref[:, cols] = acc_ref[:, cols] * keep + dot(
                val_t, weights.astype(jnp.bfloat16), ((1,), (0,))
            )

    m_ref[...] = jnp.full_like(m_ref, SCORE_FLOOR)
    l_ref[...] = jnp.zeros_like(l_ref)
    acc_ref[...] = jnp.zeros_like(acc_ref)
    first = h if native else 0
    pass_on(first, 1)
    attend(kvc[c, 0], kvc[c, 1], None)

    for off in range(1, nh):
        from_head(prx, psend, precv, off).wait_recv()
        slot = lax.rem(h + nh - off, nh)
        part[...] += prx[slot].astype(jnp.float32)
    fresh = part[...].astype(jnp.bfloat16)
    raw = dot(fresh[:, :rank], kup_ref[0], ((1,), (0,)))
    kvf[c, 0] = rope(raw, cos_f, sin_f).astype(jnp.bfloat16)
    kvf[c, 1] = dot(fresh[:, rank:], vup_ref[0], ((1,), (0,))).astype(jnp.bfloat16)
    send_own(2)
    pass_on(1 - first, 1)
    attend(kvf[c, 0], kvf[c, 1], 0)
    pass_on(2, 1)

    @pl.loop(1, n)
    def _(step):
        @pl.loop(0, 2)
        def _(side):
            span = c + step - 2 * step * side

            @pl.when(jnp.logical_and(span >= 0, span < n))
            def _():
                attend(kvc[span, 0], kvc[span, 1], None)

        @pl.when(step < n - 1)
        def _():
            pass_on(first, step + 1)
            pass_on(1 - first, step + 1)

        @pl.loop(0, 2)
        def _(side):
            span = c + step - 2 * step * side

            @pl.when(jnp.logical_and(span >= 0, span < n))
            def _():
                attend(kvf[span, 0], kvf[span, 1], (own_place - span_ref[0, span]) * fresh_dev)

        @pl.when(step < n - 1)
        def _():
            pass_on(2, step + 1)

    for g in range(per_kv):
        cols = slice(g * fresh_dev, (g + 1) * fresh_dev)
        mixed = acc_ref[:, cols] / l_ref[:, cols]
        out_ref[0, :, g * hd:(g + 1) * hd] = mixed.T.astype(out_ref.dtype)

    for off in range(1, nh):
        to_head(cache_ref.at[0], crx, csend, crecv, off).wait_send()
        to_head(pout, prx, psend, precv, off).wait_send()

    @pl.loop(0, n)
    def _(span):
        for piece in range(3):
            @pl.when(jnp.logical_and(span >= c, c > 0))
            def _():
                along(piece, span, 0).wait_send()

            @pl.when(jnp.logical_and(span <= c, c < n - 1))
            def _():
                along(piece, span, 1).wait_send()


def per_device(n, nh, fresh_hidden, latent_down, cache_latents, key_up, value_up, queries, span_start):
    fresh_dev, depth = fresh_hidden.shape[1:]
    cache_dev, cw = cache_latents.shape[1:]
    lat = latent_down.shape[1]
    hd = key_up.shape[2]
    rows = fresh_dev * (queries.shape[2] // hd)
    near, far = rope_tables(n, cache_dev, fresh_dev, hd)
    near, far = jnp.asarray(near), jnp.asarray(far)
    small = (cache_latents, key_up, value_up, queries, near, far)
    chunks = 8
    vmem = pl.BlockSpec(memory_space=pltpu.VMEM)
    hbm = pl.BlockSpec(memory_space=pltpu.HBM)
    dma = pltpu.SemaphoreType.DMA
    bf = jnp.bfloat16
    return pl.pallas_call(
        functools.partial(kernel, n=n, nh=nh, chunks=chunks),
        out_shape=jax.ShapeDtypeStruct(queries.shape, queries.dtype),
        in_specs=[pl.BlockSpec(memory_space=pltpu.SMEM)] + [hbm] * 8,
        out_specs=vmem,
        scratch_shapes=[
            *(pltpu.VMEM(x.shape, x.dtype) for x in small),
            dma((len(small),)),
            pltpu.VMEM((fresh_dev, depth), bf),
            pltpu.VMEM((depth, lat), bf),
            pltpu.VMEM((nh, cache_dev, cw), bf),
            pltpu.VMEM((fresh_dev, lat), jnp.float32),
            pltpu.VMEM((fresh_dev, lat), bf),
            pltpu.VMEM((nh, fresh_dev, lat), bf),
            pltpu.VMEM((n, 2, cache_dev, hd), bf),
            pltpu.VMEM((n, 2, fresh_dev, hd), bf),
            pltpu.VMEM((rows, hd), bf),
            pltpu.VMEM((1, rows), jnp.float32),
            pltpu.VMEM((1, rows), jnp.float32),
            pltpu.VMEM((hd, rows), jnp.float32),
            dma((chunks,)), dma((chunks,)),
            dma((nh,)), dma((nh,)), dma((nh,)), dma((nh,)),
            dma((3, 2, n)), dma((3, n)),
        ],
        compiler_params=pltpu.CompilerParams(
            collective_id=0, has_side_effects=True, vmem_limit_bytes=62 * 2 ** 20
        ),
    )(span_start, fresh_hidden, latent_down, cache_latents, key_up, value_up, queries,
      near, far)


def solution(mesh):
    return jax.shard_map(
        functools.partial(per_device, mesh.shape["ctx"], mesh.shape["head"]),
        mesh=mesh,
        in_specs=(
            P(("group", "req"), "ctx", "head"),
            P("head", None),
            P(("group", "req"), "ctx", "head"),
            P("head", None, None),
            P("head", None, None),
            P(("group", "req"), "ctx", "head"),
            P(("group", "req"), None),
        ),
        out_specs=P(("group", "req"), "ctx", "head"),
        check_vma=False,
    )
```

```python
import functools
import math

import jax
import jax.numpy as jnp
import numpy as np
from jax import lax
from jax.experimental import pallas as pl
from jax.experimental.pallas import tpu as pltpu
from jax.sharding import PartitionSpec as P

ROPE_BASE = 500000.0
SCORE_FLOOR = -1e30
MESH = pl.DeviceIdType.MESH


def rope_tables(span_count, cache_dev, fresh_dev, head_dim):
    half = head_dim // 2
    freq = ROPE_BASE ** (-(np.arange(half, dtype=np.float64) * 2.0 / head_dim))
    freq = np.concatenate([freq, freq])
    sign = np.concatenate([-np.ones(half), np.ones(half)])

    def both(positions):
        angles = positions[:, None].astype(np.float64) * freq[None, :]
        return np.stack([np.cos(angles), np.sin(angles) * sign]).astype(np.float32)

    places = np.arange(span_count)
    near = both(np.arange(max(cache_dev, fresh_dev)))
    far = np.concatenate(
        [both(places * cache_dev), both(span_count * cache_dev + places * fresh_dev)]
    )
    return near, far


def dot(a, b, dims):
    return lax.dot_general(a, b, (dims, ((), ())), preferred_element_type=jnp.float32)


def kernel(
    span_ref, hidden_hbm, down_hbm, cache_hbm, kup_hbm, vup_hbm, q_hbm, near_hbm, far_hbm,
    out_ref,
    cache_ref, kup_ref, vup_ref, q_ref, near_ref, far_ref, isem, hidden, down, crx, part, pout, prx, kvc, kvf, qrot, m_ref, l_ref, acc_ref,
    hsem, dsem, csend, crecv, psend, precv, ssem, rsem,
    *, n, nh, chunks,
):
    c = lax.axis_index("ctx")
    h = lax.axis_index("head")
    fresh_dev = q_ref.shape[1]
    cache_dev, cw = cache_ref.shape[1:]
    rank, hd = kup_ref.shape[1:]
    per_kv = q_ref.shape[2] // hd
    rows = per_kv * fresh_dev
    depth = hidden.shape[1] // chunks
    native = nh == 2 and cw == rank
    small = [
        pltpu.make_async_copy(src, dst, isem.at[i])
        for i, (src, dst) in enumerate((
            (cache_hbm, cache_ref), (kup_hbm, kup_ref), (vup_hbm, vup_ref),
            (near_hbm, near_ref), (far_hbm, far_ref), (q_hbm, q_ref),
        ))
    ]
    for one in small:
        one.start()
    loads = []
    for i in range(chunks):
        at = pl.ds(i * depth, depth)
        loads.append((
            pltpu.make_async_copy(hidden_hbm.at[0, :, at], hidden.at[:, at], hsem.at[i]),
            pltpu.make_async_copy(down_hbm.at[at, :], down.at[at, :], dsem.at[i]),
        ))
        for one in loads[-1]:
            one.start()

    barrier = pltpu.get_barrier_semaphore()
    for off in range(1, nh):
        pl.semaphore_signal(
            barrier, inc=1, device_id={"head": lax.rem(h + off, nh)}, device_id_type=MESH
        )

    @pl.when(c > 0)
    def _():
        pl.semaphore_signal(barrier, inc=1, device_id={"ctx": c - 1}, device_id_type=MESH)

    @pl.when(c < n - 1)
    def _():
        pl.semaphore_signal(barrier, inc=1, device_id={"ctx": c + 1}, device_id_type=MESH)

    inner = jnp.where(c > 0, 1, 0) + jnp.where(c < n - 1, 1, 0)
    pl.semaphore_wait(barrier, nh - 1 + inner)

    def to_head(src, dst, send, recv, off):
        return pltpu.make_async_remote_copy(
            src_ref=src, dst_ref=dst.at[h], send_sem=send.at[off], recv_sem=recv.at[h],
            device_id={"head": lax.rem(h + off, nh)}, device_id_type=MESH,
        )

    def from_head(dst, send, recv, off):
        slot = lax.rem(h + nh - off, nh)
        return pltpu.make_async_remote_copy(
            src_ref=dst.at[slot], dst_ref=dst.at[slot], send_sem=send.at[off],
            recv_sem=recv.at[slot], device_id={"head": slot}, device_id_type=MESH,
        )

    small[0].wait()
    for off in range(1, nh):
        to_head(cache_ref.at[0], crx, csend, crecv, off).start()

    def along(piece, span, side):
        if isinstance(piece, int) and piece >= 2:
            ref = kvf.at[span, piece - 2]
        else:
            ref = kvc.at[span, piece]
        there = c + 2 * side - 1
        return pltpu.make_async_remote_copy(
            src_ref=ref, dst_ref=ref, send_sem=ssem.at[piece, side, span],
            recv_sem=rsem.at[piece, span], device_id={"ctx": there}, device_id_type=MESH,
        )

    def send_own(piece):
        @pl.when(c > 0)
        def _():
            along(piece, c, 0).start()

        @pl.when(c < n - 1)
        def _():
            along(piece, c, 1).start()

    def turn(table, place):
        row = lax.broadcasted_iota(jnp.int32, (n, hd), 0)
        cos_p = jnp.sum(jnp.where(row == place, far_ref[2 * table], 0.0), axis=0, keepdims=True)
        sin_p = jnp.sum(jnp.where(row == place, far_ref[2 * table + 1], 0.0), axis=0, keepdims=True)
        count = fresh_dev if table else cache_dev
        cos_j = near_ref[0, :count]
        sin_j = near_ref[1, :count]
        return cos_j * cos_p - sin_j * sin_p, sin_j * cos_p + cos_j * sin_p

    def rope(field, cosine, signed_sine):
        return field * cosine + pltpu.roll(field, hd // 2, 1) * signed_sine

    for one in small[1:5]:
        one.wait()
    own_place = span_ref[0, c]
    cos_c, sin_c = turn(0, own_place)
    cos_f, sin_f = turn(1, own_place)

    if native:
        @pl.when(h == 0)
        def _():
            raw = dot(cache_ref[0], kup_ref[0], ((1,), (0,)))
            kvc[c, 0] = rope(raw, cos_c, sin_c).astype(jnp.bfloat16)
            send_own(0)

        @pl.when(h == 1)
        def _():
            kvc[c, 1] = dot(cache_ref[0], vup_ref[0], ((1,), (0,))).astype(jnp.bfloat16)
            send_own(1)

    for i in range(chunks):
        for one in loads[i]:
            one.wait()
        at = pl.ds(i * depth, depth)
        term = dot(hidden[:, at], down[at, :], ((1,), (0,)))
        if i == 0:
            part[...] = term
        else:
            part[...] += term
    pout[...] = part[...].astype(jnp.bfloat16)
    for off in range(1, nh):
        to_head(pout, prx, psend, precv, off).start()

    for off in range(1, nh):
        from_head(crx, csend, crecv, off).wait_recv()
    if native:
        @pl.when(h == 1)
        def _():
            raw = dot(crx[0], kup_ref[0], ((1,), (0,)))
            kvc[c, 0] = rope(raw, cos_c, sin_c).astype(jnp.bfloat16)
            send_own(0)

        @pl.when(h == 0)
        def _():
            kvc[c, 1] = dot(crx[1], vup_ref[0], ((1,), (0,))).astype(jnp.bfloat16)
            send_own(1)
    else:
        crx[h] = cache_ref[0]
        raw = jnp.zeros((cache_dev, hd), jnp.float32)
        val = jnp.zeros((cache_dev, hd), jnp.float32)
        for j in range(nh):
            at = j * cw
            if at < rank:
                raw += dot(crx[j], kup_ref[0, at:at + cw], ((1,), (0,)))
            else:
                val += dot(crx[j], vup_ref[0, at - rank:at - rank + cw], ((1,), (0,)))
        kvc[c, 0] = rope(raw, cos_c, sin_c).astype(jnp.bfloat16)
        kvc[c, 1] = val.astype(jnp.bfloat16)
        send_own(0)
        send_own(1)

    small[5].wait()
    factor = hd ** -0.5 * math.log2(math.e)
    for g in range(per_kv):
        head = q_ref[0, :, g * hd:(g + 1) * hd].astype(jnp.float32)
        qrot[g * fresh_dev:(g + 1) * fresh_dev, :] = (
            rope(head, cos_f, sin_f) * factor
        ).astype(jnp.bfloat16)

    def pass_on(piece, step):
        @pl.loop(0, 2)
        def _(side):
            span = c + step - 2 * step * side
            onward = c + 2 * side - 1
            inside = jnp.logical_and(span >= 0, span < n)

            @pl.when(inside)
            def _():
                along(piece, span, side).wait_recv()

                @pl.when(jnp.logical_and(onward >= 0, onward < n))
                def _():
                    along(piece, span, side).start()

    def attend(keys, values, shift):
        val_t = values.T
        width = min(rows, 2 * fresh_dev)
        count = keys.shape[0]

        @pl.loop(0, rows // width, unroll=True)
        def _(i):
            cols = pl.ds(pl.multiple_of(i * width, width), width)
            scores = dot(keys, qrot[cols, :], ((1,), (1,)))
            if shift is not None:
                ik = lax.broadcasted_iota(jnp.int32, (count, width), 0)
                iq = lax.broadcasted_iota(jnp.int32, (count, width), 1)
                iq = jnp.where(iq >= fresh_dev, iq - fresh_dev, iq)
                scores = jnp.where(ik - iq <= shift, scores, SCORE_FLOOR)
            old = m_ref[:, cols]
            new = jnp.maximum(old, jnp.max(scores, axis=0, keepdims=True))
            weights = jnp.exp2(scores - new)
            keep = jnp.exp2(old - new)
            m_ref[:, cols] = new
            l_ref[:, cols] = l_ref[:, cols] * keep + jnp.sum(weights, axis=0, keepdims=True)
            acc_ref[:, cols] = acc_ref[:, cols] * keep + dot(
                val_t, weights.astype(jnp.bfloat16), ((1,), (0,))
            )

    m_ref[...] = jnp.full_like(m_ref, SCORE_FLOOR)
    l_ref[...] = jnp.zeros_like(l_ref)
    acc_ref[...] = jnp.zeros_like(acc_ref)
    first = h if native else 0
    pass_on(first, 1)
    attend(kvc[c, 0], kvc[c, 1], None)

    for off in range(1, nh):
        from_head(prx, psend, precv, off).wait_recv()
        slot = lax.rem(h + nh - off, nh)
        part[...] += prx[slot].astype(jnp.float32)
    fresh = part[...].astype(jnp.bfloat16)
    raw = dot(fresh[:, :rank], kup_ref[0], ((1,), (0,)))
    kvf[c, 0] = rope(raw, cos_f, sin_f).astype(jnp.bfloat16)
    kvf[c, 1] = dot(fresh[:, rank:], vup_ref[0], ((1,), (0,))).astype(jnp.bfloat16)
    send_own(2)
    send_own(3)
    pass_on(1 - first, 1)

    @pl.loop(1, n)
    def _(step):
        @pl.loop(0, 2)
        def _(side):
            span = c + step - 2 * step * side

            @pl.when(jnp.logical_and(span >= 0, span < n))
            def _():
                attend(kvc[span, 0], kvc[span, 1], None)

        @pl.when(step < n - 1)
        def _():
            pass_on(first, step + 1)
            pass_on(1 - first, step + 1)

        @pl.when(step == 1)
        def _():
            pass_on(2, 1)
            pass_on(3, 1)

    attend(kvf[c, 0], kvf[c, 1], 0)

    @pl.loop(1, n)
    def _(step):
        @pl.loop(0, 2)
        def _(side):
            span = c + step - 2 * step * side

            @pl.when(jnp.logical_and(span >= 0, span < n))
            def _():
                attend(kvf[span, 0], kvf[span, 1], (own_place - span_ref[0, span]) * fresh_dev)

        @pl.when(step < n - 1)
        def _():
            pass_on(2, step + 1)
            pass_on(3, step + 1)

    for g in range(per_kv):
        cols = slice(g * fresh_dev, (g + 1) * fresh_dev)
        mixed = acc_ref[:, cols] / l_ref[:, cols]
        out_ref[0, :, g * hd:(g + 1) * hd] = mixed.T.astype(out_ref.dtype)

    for off in range(1, nh):
        to_head(cache_ref.at[0], crx, csend, crecv, off).wait_send()
        to_head(pout, prx, psend, precv, off).wait_send()

    @pl.loop(0, n)
    def _(span):
        for piece in range(4):
            @pl.when(jnp.logical_and(span >= c, c > 0))
            def _():
                along(piece, span, 0).wait_send()

            @pl.when(jnp.logical_and(span <= c, c < n - 1))
            def _():
                along(piece, span, 1).wait_send()


def per_device(n, nh, fresh_hidden, latent_down, cache_latents, key_up, value_up, queries, span_start):
    fresh_dev, depth = fresh_hidden.shape[1:]
    cache_dev, cw = cache_latents.shape[1:]
    lat = latent_down.shape[1]
    hd = key_up.shape[2]
    rows = fresh_dev * (queries.shape[2] // hd)
    near, far = rope_tables(n, cache_dev, fresh_dev, hd)
    near, far = jnp.asarray(near), jnp.asarray(far)
    small = (cache_latents, key_up, value_up, queries, near, far)
    chunks = 8
    vmem = pl.BlockSpec(memory_space=pltpu.VMEM)
    hbm = pl.BlockSpec(memory_space=pltpu.HBM)
    dma = pltpu.SemaphoreType.DMA
    bf = jnp.bfloat16
    return pl.pallas_call(
        functools.partial(kernel, n=n, nh=nh, chunks=chunks),
        out_shape=jax.ShapeDtypeStruct(queries.shape, queries.dtype),
        in_specs=[pl.BlockSpec(memory_space=pltpu.SMEM)] + [hbm] * 8,
        out_specs=vmem,
        scratch_shapes=[
            *(pltpu.VMEM(x.shape, x.dtype) for x in small),
            dma((len(small),)),
            pltpu.VMEM((fresh_dev, depth), bf),
            pltpu.VMEM((depth, lat), bf),
            pltpu.VMEM((nh, cache_dev, cw), bf),
            pltpu.VMEM((fresh_dev, lat), jnp.float32),
            pltpu.VMEM((fresh_dev, lat), bf),
            pltpu.VMEM((nh, fresh_dev, lat), bf),
            pltpu.VMEM((n, 2, cache_dev, hd), bf),
            pltpu.VMEM((n, 2, fresh_dev, hd), bf),
            pltpu.VMEM((rows, hd), bf),
            pltpu.VMEM((1, rows), jnp.float32),
            pltpu.VMEM((1, rows), jnp.float32),
            pltpu.VMEM((hd, rows), jnp.float32),
            dma((chunks,)), dma((chunks,)),
            dma((nh,)), dma((nh,)), dma((nh,)), dma((nh,)),
            dma((4, 2, n)), dma((4, n)),
        ],
        compiler_params=pltpu.CompilerParams(
            collective_id=0, has_side_effects=True, vmem_limit_bytes=62 * 2 ** 20
        ),
    )(span_start, fresh_hidden, latent_down, cache_latents, key_up, value_up, queries,
      near, far)


def solution(mesh):
    return jax.shard_map(
        functools.partial(per_device, mesh.shape["ctx"], mesh.shape["head"]),
        mesh=mesh,
        in_specs=(
            P(("group", "req"), "ctx", "head"),
            P("head", None),
            P(("group", "req"), "ctx", "head"),
            P("head", None, None),
            P("head", None, None),
            P(("group", "req"), "ctx", "head"),
            P(("group", "req"), None),
        ),
        out_specs=P(("group", "req"), "ctx", "head"),
        check_vma=False,
    )
```

```python
import functools
import math

import jax
import jax.numpy as jnp
import numpy as np
from jax import lax
from jax.experimental import pallas as pl
from jax.experimental.pallas import tpu as pltpu
from jax.sharding import PartitionSpec as P

ROPE_BASE = 500000.0
SCORE_FLOOR = -1e30
MESH = pl.DeviceIdType.MESH


def rope_tables(span_count, cache_dev, fresh_dev, head_dim):
    half = head_dim // 2
    freq = ROPE_BASE ** (-(np.arange(half, dtype=np.float64) * 2.0 / head_dim))
    freq = np.concatenate([freq, freq])
    sign = np.concatenate([-np.ones(half), np.ones(half)])

    def both(positions):
        angles = positions[:, None].astype(np.float64) * freq[None, :]
        return np.stack([np.cos(angles), np.sin(angles) * sign]).astype(np.float32)

    places = np.arange(span_count)
    near = both(np.arange(max(cache_dev, fresh_dev)))
    far = np.concatenate(
        [both(places * cache_dev), both(span_count * cache_dev + places * fresh_dev)]
    )
    return near, far


def dot(a, b, dims):
    return lax.dot_general(a, b, (dims, ((), ())), preferred_element_type=jnp.float32)


def kernel(
    span_ref, hidden_hbm, down_hbm, cache_hbm, kup_hbm, vup_hbm, q_hbm, near_hbm, far_hbm,
    out_ref,
    cache_ref, kup_ref, vup_ref, q_ref, near_ref, far_ref, isem, hidden, down, crx, part, pout, prx, kvc, kvf, qrot, m_ref, l_ref, acc_ref,
    hsem, dsem, csend, crecv, psend, precv, ssem, rsem,
    *, n, nh, chunks,
):
    c = lax.axis_index("ctx")
    h = lax.axis_index("head")
    fresh_dev = q_ref.shape[1]
    cache_dev, cw = cache_ref.shape[1:]
    rank, hd = kup_ref.shape[1:]
    per_kv = q_ref.shape[2] // hd
    rows = per_kv * fresh_dev
    depth = hidden.shape[1] // chunks
    native = nh == 2 and cw == rank
    small = [
        pltpu.make_async_copy(src, dst, isem.at[i])
        for i, (src, dst) in enumerate((
            (cache_hbm, cache_ref), (kup_hbm, kup_ref), (vup_hbm, vup_ref),
            (near_hbm, near_ref), (far_hbm, far_ref), (q_hbm, q_ref),
        ))
    ]
    for one in small:
        one.start()
    loads = []
    for i in range(chunks):
        at = pl.ds(i * depth, depth)
        loads.append((
            pltpu.make_async_copy(hidden_hbm.at[0, :, at], hidden.at[:, at], hsem.at[i]),
            pltpu.make_async_copy(down_hbm.at[at, :], down.at[at, :], dsem.at[i]),
        ))
        for one in loads[-1]:
            one.start()

    barrier = pltpu.get_barrier_semaphore()
    for off in range(1, nh):
        pl.semaphore_signal(
            barrier, inc=1, device_id={"head": lax.rem(h + off, nh)}, device_id_type=MESH
        )

    @pl.when(c > 0)
    def _():
        pl.semaphore_signal(barrier, inc=1, device_id={"ctx": c - 1}, device_id_type=MESH)

    @pl.when(c < n - 1)
    def _():
        pl.semaphore_signal(barrier, inc=1, device_id={"ctx": c + 1}, device_id_type=MESH)

    inner = jnp.where(c > 0, 1, 0) + jnp.where(c < n - 1, 1, 0)
    pl.semaphore_wait(barrier, nh - 1 + inner)

    def to_head(src, dst, send, recv, off):
        return pltpu.make_async_remote_copy(
            src_ref=src, dst_ref=dst.at[h], send_sem=send.at[off], recv_sem=recv.at[h],
            device_id={"head": lax.rem(h + off, nh)}, device_id_type=MESH,
        )

    def from_head(dst, send, recv, off):
        slot = lax.rem(h + nh - off, nh)
        return pltpu.make_async_remote_copy(
            src_ref=dst.at[slot], dst_ref=dst.at[slot], send_sem=send.at[off],
            recv_sem=recv.at[slot], device_id={"head": slot}, device_id_type=MESH,
        )

    small[0].wait()
    for off in range(1, nh):
        to_head(cache_ref.at[0], crx, csend, crecv, off).start()

    def along(piece, span, side):
        if isinstance(piece, int) and piece >= 2:
            ref = kvf.at[span, piece - 2]
        else:
            ref = kvc.at[span, piece]
        there = c + 2 * side - 1
        return pltpu.make_async_remote_copy(
            src_ref=ref, dst_ref=ref, send_sem=ssem.at[piece, side, span],
            recv_sem=rsem.at[piece, span], device_id={"ctx": there}, device_id_type=MESH,
        )

    def send_own(piece):
        @pl.when(c > 0)
        def _():
            along(piece, c, 0).start()

        @pl.when(c < n - 1)
        def _():
            along(piece, c, 1).start()

    def turn(table, place):
        row = lax.broadcasted_iota(jnp.int32, (n, hd), 0)
        cos_p = jnp.sum(jnp.where(row == place, far_ref[2 * table], 0.0), axis=0, keepdims=True)
        sin_p = jnp.sum(jnp.where(row == place, far_ref[2 * table + 1], 0.0), axis=0, keepdims=True)
        count = fresh_dev if table else cache_dev
        cos_j = near_ref[0, :count]
        sin_j = near_ref[1, :count]
        return cos_j * cos_p - sin_j * sin_p, sin_j * cos_p + cos_j * sin_p

    def rope(field, cosine, signed_sine):
        return field * cosine + pltpu.roll(field, hd // 2, 1) * signed_sine

    for one in small[1:5]:
        one.wait()
    own_place = span_ref[0, c]
    cos_c, sin_c = turn(0, own_place)
    cos_f, sin_f = turn(1, own_place)

    if native:
        @pl.when(h == 0)
        def _():
            raw = dot(cache_ref[0], kup_ref[0], ((1,), (0,)))
            kvc[c, 0] = rope(raw, cos_c, sin_c).astype(jnp.bfloat16)
            send_own(0)

        @pl.when(h == 1)
        def _():
            kvc[c, 1] = dot(cache_ref[0], vup_ref[0], ((1,), (0,))).astype(jnp.bfloat16)
            send_own(1)

    small[5].wait()
    factor = hd ** -0.5 * math.log2(math.e)
    for g in range(per_kv):
        head = q_ref[0, :, g * hd:(g + 1) * hd].astype(jnp.float32)
        qrot[g * fresh_dev:(g + 1) * fresh_dev, :] = (
            rope(head, cos_f, sin_f) * factor
        ).astype(jnp.bfloat16)

    for i in range(chunks):
        for one in loads[i]:
            one.wait()
        at = pl.ds(i * depth, depth)
        term = dot(hidden[:, at], down[at, :], ((1,), (0,)))
        if i == 0:
            part[...] = term
        else:
            part[...] += term
    pout[...] = part[...].astype(jnp.bfloat16)
    for off in range(1, nh):
        to_head(pout, prx, psend, precv, off).start()

    for off in range(1, nh):
        from_head(crx, csend, crecv, off).wait_recv()
    if native:
        @pl.when(h == 1)
        def _():
            raw = dot(crx[0], kup_ref[0], ((1,), (0,)))
            kvc[c, 0] = rope(raw, cos_c, sin_c).astype(jnp.bfloat16)
            send_own(0)

        @pl.when(h == 0)
        def _():
            kvc[c, 1] = dot(crx[1], vup_ref[0], ((1,), (0,))).astype(jnp.bfloat16)
            send_own(1)
    else:
        crx[h] = cache_ref[0]
        raw = jnp.zeros((cache_dev, hd), jnp.float32)
        val = jnp.zeros((cache_dev, hd), jnp.float32)
        for j in range(nh):
            at = j * cw
            if at < rank:
                raw += dot(crx[j], kup_ref[0, at:at + cw], ((1,), (0,)))
            else:
                val += dot(crx[j], vup_ref[0, at - rank:at - rank + cw], ((1,), (0,)))
        kvc[c, 0] = rope(raw, cos_c, sin_c).astype(jnp.bfloat16)
        kvc[c, 1] = val.astype(jnp.bfloat16)
        send_own(0)
        send_own(1)

    def pass_on(piece, step):
        @pl.loop(0, 2)
        def _(side):
            span = c + step - 2 * step * side
            onward = c + 2 * side - 1
            inside = jnp.logical_and(span >= 0, span < n)

            @pl.when(inside)
            def _():
                along(piece, span, side).wait_recv()

                @pl.when(jnp.logical_and(onward >= 0, onward < n))
                def _():
                    along(piece, span, side).start()

    def attend(keys, values, shift):
        val_t = values.T
        width = min(rows, 2 * fresh_dev)
        count = keys.shape[0]

        @pl.loop(0, rows // width, unroll=True)
        def _(i):
            cols = pl.ds(pl.multiple_of(i * width, width), width)
            scores = dot(keys, qrot[cols, :], ((1,), (1,)))
            if shift is not None:
                ik = lax.broadcasted_iota(jnp.int32, (count, width), 0)
                iq = lax.broadcasted_iota(jnp.int32, (count, width), 1)
                iq = jnp.where(iq >= fresh_dev, iq - fresh_dev, iq)
                scores = jnp.where(ik - iq <= shift, scores, SCORE_FLOOR)
            old = m_ref[:, cols]
            new = jnp.maximum(old, jnp.max(scores, axis=0, keepdims=True))
            weights = jnp.exp2(scores - new)
            keep = jnp.exp2(old - new)
            m_ref[:, cols] = new
            l_ref[:, cols] = l_ref[:, cols] * keep + jnp.sum(weights, axis=0, keepdims=True)
            acc_ref[:, cols] = acc_ref[:, cols] * keep + dot(
                val_t, weights.astype(jnp.bfloat16), ((1,), (0,))
            )

    m_ref[...] = jnp.full_like(m_ref, SCORE_FLOOR)
    l_ref[...] = jnp.zeros_like(l_ref)
    acc_ref[...] = jnp.zeros_like(acc_ref)
    first = h if native else 0
    pass_on(first, 1)
    attend(kvc[c, 0], kvc[c, 1], None)

    for off in range(1, nh):
        from_head(prx, psend, precv, off).wait_recv()
        slot = lax.rem(h + nh - off, nh)
        part[...] += prx[slot].astype(jnp.float32)
    fresh = part[...].astype(jnp.bfloat16)
    raw = dot(fresh[:, :rank], kup_ref[0], ((1,), (0,)))
    kvf[c, 0] = rope(raw, cos_f, sin_f).astype(jnp.bfloat16)
    kvf[c, 1] = dot(fresh[:, rank:], vup_ref[0], ((1,), (0,))).astype(jnp.bfloat16)
    send_own(2)
    send_own(3)
    pass_on(1 - first, 1)

    @pl.loop(1, n)
    def _(step):
        @pl.loop(0, 2)
        def _(side):
            span = c + step - 2 * step * side

            @pl.when(jnp.logical_and(span >= 0, span < n))
            def _():
                attend(kvc[span, 0], kvc[span, 1], None)

        @pl.when(step < n - 1)
        def _():
            pass_on(first, step + 1)
            pass_on(1 - first, step + 1)

        @pl.when(step == 1)
        def _():
            pass_on(2, 1)
            pass_on(3, 1)

    attend(kvf[c, 0], kvf[c, 1], 0)

    @pl.loop(1, n)
    def _(step):
        @pl.loop(0, 2)
        def _(side):
            span = c + step - 2 * step * side

            @pl.when(jnp.logical_and(span >= 0, span < n))
            def _():
                attend(kvf[span, 0], kvf[span, 1], (own_place - span_ref[0, span]) * fresh_dev)

        @pl.when(step < n - 1)
        def _():
            pass_on(2, step + 1)
            pass_on(3, step + 1)

    for g in range(per_kv):
        cols = slice(g * fresh_dev, (g + 1) * fresh_dev)
        mixed = acc_ref[:, cols] / l_ref[:, cols]
        out_ref[0, :, g * hd:(g + 1) * hd] = mixed.T.astype(out_ref.dtype)

    for off in range(1, nh):
        to_head(cache_ref.at[0], crx, csend, crecv, off).wait_send()
        to_head(pout, prx, psend, precv, off).wait_send()

    @pl.loop(0, n)
    def _(span):
        for piece in range(4):
            @pl.when(jnp.logical_and(span >= c, c > 0))
            def _():
                along(piece, span, 0).wait_send()

            @pl.when(jnp.logical_and(span <= c, c < n - 1))
            def _():
                along(piece, span, 1).wait_send()


def per_device(n, nh, fresh_hidden, latent_down, cache_latents, key_up, value_up, queries, span_start):
    fresh_dev, depth = fresh_hidden.shape[1:]
    cache_dev, cw = cache_latents.shape[1:]
    lat = latent_down.shape[1]
    hd = key_up.shape[2]
    rows = fresh_dev * (queries.shape[2] // hd)
    near, far = rope_tables(n, cache_dev, fresh_dev, hd)
    near, far = jnp.asarray(near), jnp.asarray(far)
    small = (cache_latents, key_up, value_up, queries, near, far)
    chunks = 8
    vmem = pl.BlockSpec(memory_space=pltpu.VMEM)
    hbm = pl.BlockSpec(memory_space=pltpu.HBM)
    dma = pltpu.SemaphoreType.DMA
    bf = jnp.bfloat16
    return pl.pallas_call(
        functools.partial(kernel, n=n, nh=nh, chunks=chunks),
        out_shape=jax.ShapeDtypeStruct(queries.shape, queries.dtype),
        in_specs=[pl.BlockSpec(memory_space=pltpu.SMEM)] + [hbm] * 8,
        out_specs=vmem,
        scratch_shapes=[
            *(pltpu.VMEM(x.shape, x.dtype) for x in small),
            dma((len(small),)),
            pltpu.VMEM((fresh_dev, depth), bf),
            pltpu.VMEM((depth, lat), bf),
            pltpu.VMEM((nh, cache_dev, cw), bf),
            pltpu.VMEM((fresh_dev, lat), jnp.float32),
            pltpu.VMEM((fresh_dev, lat), bf),
            pltpu.VMEM((nh, fresh_dev, lat), bf),
            pltpu.VMEM((n, 2, cache_dev, hd), bf),
            pltpu.VMEM((n, 2, fresh_dev, hd), bf),
            pltpu.VMEM((rows, hd), bf),
            pltpu.VMEM((1, rows), jnp.float32),
            pltpu.VMEM((1, rows), jnp.float32),
            pltpu.VMEM((hd, rows), jnp.float32),
            dma((chunks,)), dma((chunks,)),
            dma((nh,)), dma((nh,)), dma((nh,)), dma((nh,)),
            dma((4, 2, n)), dma((4, n)),
        ],
        compiler_params=pltpu.CompilerParams(
            collective_id=0, has_side_effects=True, vmem_limit_bytes=62 * 2 ** 20
        ),
    )(span_start, fresh_hidden, latent_down, cache_latents, key_up, value_up, queries,
      near, far)


def solution(mesh):
    return jax.shard_map(
        functools.partial(per_device, mesh.shape["ctx"], mesh.shape["head"]),
        mesh=mesh,
        in_specs=(
            P(("group", "req"), "ctx", "head"),
            P("head", None),
            P(("group", "req"), "ctx", "head"),
            P("head", None, None),
            P("head", None, None),
            P(("group", "req"), "ctx", "head"),
            P(("group", "req"), None),
        ),
        out_specs=P(("group", "req"), "ctx", "head"),
        check_vma=False,
    )
```

```python
import functools
import math

import jax
import jax.numpy as jnp
import numpy as np
from jax import lax
from jax.experimental import pallas as pl
from jax.experimental.pallas import tpu as pltpu
from jax.sharding import PartitionSpec as P

ROPE_BASE = 500000.0
SCORE_FLOOR = -1e30
MESH = pl.DeviceIdType.MESH


def rope_tables(span_count, cache_dev, fresh_dev, head_dim):
    half = head_dim // 2
    freq = ROPE_BASE ** (-(np.arange(half, dtype=np.float64) * 2.0 / head_dim))
    freq = np.concatenate([freq, freq])
    sign = np.concatenate([-np.ones(half), np.ones(half)])

    def both(positions):
        angles = positions[:, None].astype(np.float64) * freq[None, :]
        return np.stack([np.cos(angles), np.sin(angles) * sign]).astype(np.float32)

    places = np.arange(span_count)
    near = both(np.arange(max(cache_dev, fresh_dev)))
    far = np.concatenate(
        [both(places * cache_dev), both(span_count * cache_dev + places * fresh_dev)]
    )
    return near, far


def dot(a, b, dims):
    return lax.dot_general(a, b, (dims, ((), ())), preferred_element_type=jnp.float32)


def kernel(
    span_ref, hidden_hbm, down_hbm, cache_hbm, kup_hbm, vup_hbm, q_hbm, near_hbm, far_hbm,
    out_ref,
    cache_ref, kup_ref, vup_ref, q_ref, near_ref, far_ref, isem, hidden, down, crx, part, pout, prx, kvc, kvf, qrot, m_ref, l_ref, acc_ref,
    hsem, dsem, csend, crecv, psend, precv, ssem, rsem,
    *, n, nh, chunks,
):
    c = lax.axis_index("ctx")
    h = lax.axis_index("head")
    fresh_dev = q_ref.shape[1]
    cache_dev, cw = cache_ref.shape[1:]
    rank, hd = kup_ref.shape[1:]
    per_kv = q_ref.shape[2] // hd
    rows = per_kv * fresh_dev
    depth = hidden.shape[1] // chunks
    native = nh == 2 and cw == rank
    small = [
        pltpu.make_async_copy(src, dst, isem.at[i])
        for i, (src, dst) in enumerate((
            (cache_hbm, cache_ref), (kup_hbm, kup_ref), (vup_hbm, vup_ref),
            (near_hbm, near_ref), (far_hbm, far_ref), (q_hbm, q_ref),
        ))
    ]
    for one in small:
        one.start()
    loads = []
    for i in range(chunks):
        at = pl.ds(i * depth, depth)
        loads.append((
            pltpu.make_async_copy(hidden_hbm.at[0, :, at], hidden.at[:, at], hsem.at[i]),
            pltpu.make_async_copy(down_hbm.at[at, :], down.at[at, :], dsem.at[i]),
        ))
        for one in loads[-1]:
            one.start()

    barrier = pltpu.get_barrier_semaphore()
    for off in range(1, nh):
        pl.semaphore_signal(
            barrier, inc=1, device_id={"head": lax.rem(h + off, nh)}, device_id_type=MESH
        )

    @pl.when(c > 0)
    def _():
        pl.semaphore_signal(barrier, inc=1, device_id={"ctx": c - 1}, device_id_type=MESH)

    @pl.when(c < n - 1)
    def _():
        pl.semaphore_signal(barrier, inc=1, device_id={"ctx": c + 1}, device_id_type=MESH)

    inner = jnp.where(c > 0, 1, 0) + jnp.where(c < n - 1, 1, 0)
    pl.semaphore_wait(barrier, nh - 1 + inner)

    def to_head(src, dst, send, recv, off):
        return pltpu.make_async_remote_copy(
            src_ref=src, dst_ref=dst.at[h], send_sem=send.at[off], recv_sem=recv.at[h],
            device_id={"head": lax.rem(h + off, nh)}, device_id_type=MESH,
        )

    def from_head(dst, send, recv, off):
        slot = lax.rem(h + nh - off, nh)
        return pltpu.make_async_remote_copy(
            src_ref=dst.at[slot], dst_ref=dst.at[slot], send_sem=send.at[off],
            recv_sem=recv.at[slot], device_id={"head": slot}, device_id_type=MESH,
        )

    small[0].wait()
    for off in range(1, nh):
        to_head(cache_ref.at[0], crx, csend, crecv, off).start()

    def along(piece, span, side):
        if isinstance(piece, int) and piece >= 2:
            ref = kvf.at[span, piece - 2]
        else:
            ref = kvc.at[span, piece]
        there = c + 2 * side - 1
        return pltpu.make_async_remote_copy(
            src_ref=ref, dst_ref=ref, send_sem=ssem.at[piece, side, span],
            recv_sem=rsem.at[piece, span], device_id={"ctx": there}, device_id_type=MESH,
        )

    def send_own(piece):
        @pl.when(c > 0)
        def _():
            along(piece, c, 0).start()

        @pl.when(c < n - 1)
        def _():
            along(piece, c, 1).start()

    def turn(table, place):
        row = lax.broadcasted_iota(jnp.int32, (n, hd), 0)
        cos_p = jnp.sum(jnp.where(row == place, far_ref[2 * table], 0.0), axis=0, keepdims=True)
        sin_p = jnp.sum(jnp.where(row == place, far_ref[2 * table + 1], 0.0), axis=0, keepdims=True)
        count = fresh_dev if table else cache_dev
        cos_j = near_ref[0, :count]
        sin_j = near_ref[1, :count]
        return cos_j * cos_p - sin_j * sin_p, sin_j * cos_p + cos_j * sin_p

    def rope(field, cosine, signed_sine):
        return field * cosine + pltpu.roll(field, hd // 2, 1) * signed_sine

    for one in small[1:5]:
        one.wait()
    own_place = span_ref[0, c]
    cos_c, sin_c = turn(0, own_place)
    cos_f, sin_f = turn(1, own_place)

    if native:
        @pl.when(h == 0)
        def _():
            raw = dot(cache_ref[0], kup_ref[0], ((1,), (0,)))
            kvc[c, 0] = rope(raw, cos_c, sin_c).astype(jnp.bfloat16)
            send_own(0)

        @pl.when(h == 1)
        def _():
            kvc[c, 1] = dot(cache_ref[0], vup_ref[0], ((1,), (0,))).astype(jnp.bfloat16)
            send_own(1)

    small[5].wait()
    factor = hd ** -0.5 * math.log2(math.e)
    for g in range(per_kv):
        head = q_ref[0, :, g * hd:(g + 1) * hd].astype(jnp.float32)
        qrot[g * fresh_dev:(g + 1) * fresh_dev, :] = (
            rope(head, cos_f, sin_f) * factor
        ).astype(jnp.bfloat16)

    for i in range(chunks):
        for one in loads[i]:
            one.wait()
        at = pl.ds(i * depth, depth)
        term = dot(hidden[:, at], down[at, :], ((1,), (0,)))
        if i == 0:
            part[...] = term
        else:
            part[...] += term
    pout[...] = part[...].astype(jnp.bfloat16)
    for off in range(1, nh):
        to_head(pout, prx, psend, precv, off).start()

    for off in range(1, nh):
        from_head(crx, csend, crecv, off).wait_recv()
    if native:
        @pl.when(h == 1)
        def _():
            raw = dot(crx[0], kup_ref[0], ((1,), (0,)))
            kvc[c, 0] = rope(raw, cos_c, sin_c).astype(jnp.bfloat16)
            send_own(0)

        @pl.when(h == 0)
        def _():
            kvc[c, 1] = dot(crx[1], vup_ref[0], ((1,), (0,))).astype(jnp.bfloat16)
            send_own(1)
    else:
        crx[h] = cache_ref[0]
        raw = jnp.zeros((cache_dev, hd), jnp.float32)
        val = jnp.zeros((cache_dev, hd), jnp.float32)
        for j in range(nh):
            at = j * cw
            if at < rank:
                raw += dot(crx[j], kup_ref[0, at:at + cw], ((1,), (0,)))
            else:
                val += dot(crx[j], vup_ref[0, at - rank:at - rank + cw], ((1,), (0,)))
        kvc[c, 0] = rope(raw, cos_c, sin_c).astype(jnp.bfloat16)
        kvc[c, 1] = val.astype(jnp.bfloat16)
        send_own(0)
        send_own(1)

    def pass_on(piece, step):
        @pl.loop(0, 2)
        def _(side):
            span = c + step - 2 * step * side
            onward = c + 2 * side - 1
            inside = jnp.logical_and(span >= 0, span < n)

            @pl.when(inside)
            def _():
                along(piece, span, side).wait_recv()

                @pl.when(jnp.logical_and(onward >= 0, onward < n))
                def _():
                    along(piece, span, side).start()

    def attend(keys, values, shift):
        val_t = values.T
        width = min(rows, 2 * fresh_dev)
        count = keys.shape[0]

        @pl.loop(0, rows // width, unroll=True)
        def _(i):
            cols = pl.ds(pl.multiple_of(i * width, width), width)
            scores = dot(keys, qrot[cols, :], ((1,), (1,)))
            if shift is not None:
                ik = lax.broadcasted_iota(jnp.int32, (count, width), 0)
                iq = lax.broadcasted_iota(jnp.int32, (count, width), 1)
                iq = jnp.where(iq >= fresh_dev, iq - fresh_dev, iq)
                scores = jnp.where(ik - iq <= shift, scores, SCORE_FLOOR)
            old = m_ref[:, cols]
            new = jnp.maximum(old, jnp.max(scores, axis=0, keepdims=True))
            weights = jnp.exp2(scores - new)
            keep = jnp.exp2(old - new)
            m_ref[:, cols] = new
            l_ref[:, cols] = l_ref[:, cols] * keep + jnp.sum(weights, axis=0, keepdims=True)
            acc_ref[:, cols] = acc_ref[:, cols] * keep + dot(
                val_t, weights.astype(jnp.bfloat16), ((1,), (0,))
            )

    m_ref[...] = jnp.full_like(m_ref, SCORE_FLOOR)
    l_ref[...] = jnp.zeros_like(l_ref)
    acc_ref[...] = jnp.zeros_like(acc_ref)
    first = h if native else 0
    pass_on(first, 1)
    attend(kvc[c, 0], kvc[c, 1], None)

    for off in range(1, nh):
        from_head(prx, psend, precv, off).wait_recv()
        slot = lax.rem(h + nh - off, nh)
        part[...] += prx[slot].astype(jnp.float32)
    fresh = part[...].astype(jnp.bfloat16)
    raw = dot(fresh[:, :rank], kup_ref[0], ((1,), (0,)))
    kvf[c, 0] = rope(raw, cos_f, sin_f).astype(jnp.bfloat16)
    send_own(2)
    kvf[c, 1] = dot(fresh[:, rank:], vup_ref[0], ((1,), (0,))).astype(jnp.bfloat16)
    send_own(3)
    pass_on(1 - first, 1)

    @pl.loop(1, n)
    def _(step):
        @pl.loop(0, 2)
        def _(side):
            span = c + step - 2 * step * side

            @pl.when(jnp.logical_and(span >= 0, span < n))
            def _():
                attend(kvc[span, 0], kvc[span, 1], None)

        @pl.when(step < n - 1)
        def _():
            pass_on(first, step + 1)
            pass_on(1 - first, step + 1)

        @pl.when(step == 1)
        def _():
            pass_on(2, 1)
            pass_on(3, 1)

    attend(kvf[c, 0], kvf[c, 1], 0)

    @pl.loop(1, n)
    def _(step):
        @pl.loop(0, 2)
        def _(side):
            span = c + step - 2 * step * side

            @pl.when(jnp.logical_and(span >= 0, span < n))
            def _():
                attend(kvf[span, 0], kvf[span, 1], (own_place - span_ref[0, span]) * fresh_dev)

        @pl.when(step < n - 1)
        def _():
            pass_on(2, step + 1)
            pass_on(3, step + 1)

    for g in range(per_kv):
        cols = slice(g * fresh_dev, (g + 1) * fresh_dev)
        mixed = acc_ref[:, cols] / l_ref[:, cols]
        out_ref[0, :, g * hd:(g + 1) * hd] = mixed.T.astype(out_ref.dtype)

    for off in range(1, nh):
        to_head(cache_ref.at[0], crx, csend, crecv, off).wait_send()
        to_head(pout, prx, psend, precv, off).wait_send()

    @pl.loop(0, n)
    def _(span):
        for piece in range(4):
            @pl.when(jnp.logical_and(span >= c, c > 0))
            def _():
                along(piece, span, 0).wait_send()

            @pl.when(jnp.logical_and(span <= c, c < n - 1))
            def _():
                along(piece, span, 1).wait_send()


def per_device(n, nh, fresh_hidden, latent_down, cache_latents, key_up, value_up, queries, span_start):
    fresh_dev, depth = fresh_hidden.shape[1:]
    cache_dev, cw = cache_latents.shape[1:]
    lat = latent_down.shape[1]
    hd = key_up.shape[2]
    rows = fresh_dev * (queries.shape[2] // hd)
    near, far = rope_tables(n, cache_dev, fresh_dev, hd)
    near, far = jnp.asarray(near), jnp.asarray(far)
    small = (cache_latents, key_up, value_up, queries, near, far)
    chunks = 8
    vmem = pl.BlockSpec(memory_space=pltpu.VMEM)
    hbm = pl.BlockSpec(memory_space=pltpu.HBM)
    dma = pltpu.SemaphoreType.DMA
    bf = jnp.bfloat16
    return pl.pallas_call(
        functools.partial(kernel, n=n, nh=nh, chunks=chunks),
        out_shape=jax.ShapeDtypeStruct(queries.shape, queries.dtype),
        in_specs=[pl.BlockSpec(memory_space=pltpu.SMEM)] + [hbm] * 8,
        out_specs=vmem,
        scratch_shapes=[
            *(pltpu.VMEM(x.shape, x.dtype) for x in small),
            dma((len(small),)),
            pltpu.VMEM((fresh_dev, depth), bf),
            pltpu.VMEM((depth, lat), bf),
            pltpu.VMEM((nh, cache_dev, cw), bf),
            pltpu.VMEM((fresh_dev, lat), jnp.float32),
            pltpu.VMEM((fresh_dev, lat), bf),
            pltpu.VMEM((nh, fresh_dev, lat), bf),
            pltpu.VMEM((n, 2, cache_dev, hd), bf),
            pltpu.VMEM((n, 2, fresh_dev, hd), bf),
            pltpu.VMEM((rows, hd), bf),
            pltpu.VMEM((1, rows), jnp.float32),
            pltpu.VMEM((1, rows), jnp.float32),
            pltpu.VMEM((hd, rows), jnp.float32),
            dma((chunks,)), dma((chunks,)),
            dma((nh,)), dma((nh,)), dma((nh,)), dma((nh,)),
            dma((4, 2, n)), dma((4, n)),
        ],
        compiler_params=pltpu.CompilerParams(
            collective_id=0, has_side_effects=True, vmem_limit_bytes=62 * 2 ** 20
        ),
    )(span_start, fresh_hidden, latent_down, cache_latents, key_up, value_up, queries,
      near, far)


def solution(mesh):
    return jax.shard_map(
        functools.partial(per_device, mesh.shape["ctx"], mesh.shape["head"]),
        mesh=mesh,
        in_specs=(
            P(("group", "req"), "ctx", "head"),
            P("head", None),
            P(("group", "req"), "ctx", "head"),
            P("head", None, None),
            P("head", None, None),
            P(("group", "req"), "ctx", "head"),
            P(("group", "req"), None),
        ),
        out_specs=P(("group", "req"), "ctx", "head"),
        check_vma=False,
    )
```
